32 devices in a mesh: parts: 2 (over x), items: 16 (over z, y, core).
Axes of the slice: x: 2, y: 2, z: 4, core: 2. Of those that a mesh axis runs over, the one named last changes fastest.
Arguments:
- user_emb: bfloat16 [4, 64, 1024], P(None, ('parts', 'items')), parts along dimension 1
- user_gate: bfloat16 [4, 64, 64], P(None, ('parts', 'items')), parts along dimension 1
- item_table: bfloat16 [16384, 1024], P(('parts', 'items')), parts along dimension 0
- item_gate: bfloat16 [16384, 64], P(('parts', 'items')), parts along dimension 0, may hold values from -6 to 6
- cand_ids: int32 [4, 8192], P(None, ('parts', 'items')), parts along dimension 1, may hold values from 0 to 8191, as said below
- positives: int32 [4, 64], P(None, 'parts'), parts along dimension 1, may hold values from 0 to 4095
- loss_weight: float32 [4, 64], P(None, 'parts'), parts along dimension 1, may hold values from 1 to 8
- w_in: float32 [64, 128], replicated, may hold values from -0.75 to 0.75
- b_in: float32 [128], replicated, may hold values from -4 to 4
- w_out: float32 [128, 8], replicated, may hold values from -1.5 to 1.5
- b_out: float32 [8], replicated, may hold values from -4 to 4
Outputs:
- user_emb_grad: float32 [4, 64, 1024], P(None, ('parts', 'items')), parts along dimension 1
- user_gate_grad: float32 [4, 64, 64], P(None, ('parts', 'items')), parts along dimension 1
- item_table_grad: float32 [16384, 1024], P(('parts', 'items')), parts along dimension 0
- item_gate_grad: float32 [16384, 64], P(('parts', 'items')), parts along dimension 0
The draws below stay inside these ranges and needn't reach their ends.
There are 2 independent parts, one for each index of `parts`. The reference program is written for one: setup_inputs(seed, part) draws one part's arguments, and reference() takes and returns one part's arrays. A program takes and returns all parts, laid end to end along the dimension named above; an argument that names none is the same for every part. Nothing has to cross between parts.
Inputs may be any that keep to these rules, and one draw needn't show every extreme that they name: `cand_ids`: in each round, the ids at positions j * 256 to (j + 1) * 256 - 1 are distinct rows of the j-th block of 512 table rows.
All inputs are finite; a program needn't handle non-finite values.
Results may differ from the reference program's by a relative error of at most 0.0031.
Values may be sent and summed in bfloat16 or wider, within the bound.
A program may use at most 64 MiB of HBM per device.

```python
import math
import jax
import jax.numpy as jnp
from jax import lax

K = 8
E = 1024
G = 64
H = 128
ROUNDS = 4
IT_DEV = 256
TROWS_DEV = 512
USERS = 32
NC = 4096
NI = 8192


def candidate_layout(key):
    blocks = NI // TROWS_DEV
    base = jax.random.fold_in(key, 7)
    first_key, second_key = jax.random.split(base)
    raw = jax.random.randint(first_key, (ROUNDS, blocks, TROWS_DEV - 1), 0, 2 ** 18)
    order = jnp.argsort(raw * TROWS_DEV + jnp.arange(TROWS_DEV - 1, dtype=jnp.int32), axis=-1).astype(jnp.int32)
    picked = order[:, :, :IT_DEV - 1]
    last_row = jnp.full((ROUNDS, blocks, 1), TROWS_DEV - 1, jnp.int32)
    rows = jnp.concatenate([picked, last_row], axis=-1)
    mixing = jax.random.randint(second_key, (ROUNDS, blocks, IT_DEV), 0, 2 ** 18)
    shuffle = jnp.argsort(mixing * IT_DEV + jnp.arange(IT_DEV, dtype=jnp.int32), axis=-1).astype(jnp.int32)
    rows = jnp.take_along_axis(rows, shuffle, axis=-1)
    rows = rows + (jnp.arange(blocks, dtype=jnp.int32) * TROWS_DEV)[None, :, None]
    return rows.reshape(ROUNDS, NC).astype(jnp.int32)


def table_values(key):
    table_key = jax.random.fold_in(key, 11)
    values = jnp.clip(1.2 * jax.random.normal(table_key, (NI, E), jnp.float32), -7.2, 7.2)
    return values


def draw_item_table(key, part):
    return table_values(key).astype(jnp.bfloat16)


def draw_cand_ids(key, part):
    return candidate_layout(key)


def draw_user_emb(key, part):
    user_key = jax.random.fold_in(key, 13)
    base_key = jax.random.fold_in(user_key, 0)
    values = jnp.clip(1.2 * jax.random.normal(base_key, (ROUNDS, USERS, E), jnp.float32), -7.2, 7.2)
    return values.astype(jnp.bfloat16)


def draw_user_gate(key, part):
    gate_key = jax.random.fold_in(key, 17)
    base_key = jax.random.fold_in(gate_key, 0)
    values = jnp.clip(jax.random.normal(base_key, (ROUNDS, USERS, G), jnp.float32), -6.0, 6.0)
    return values.astype(jnp.bfloat16)


def touch_ends(entries, stream_key, low, largest):
    dims = entries.shape
    place = [jax.random.randint(jax.random.fold_in(stream_key, axis), (), 0, dims[axis]) for axis in range(len(dims))]
    entries = entries.at[tuple(place)].set(low)
    longest = dims.index(max(dims))
    place[longest] = (place[longest] + 1) % dims[longest]
    return entries.at[tuple(place)].set(largest)


def steps_of(key, extent, cuts, low, high):
    loudness = 1.0
    for dim, blocks in cuts:
        heights = jax.random.uniform(jax.random.fold_in(jax.random.fold_in(key, 6), dim), (blocks,), jnp.float32, low / len(cuts), high / len(cuts))
        loudness = loudness * jnp.repeat(jnp.exp(heights), extent[dim] // blocks).reshape((-1,) + (1,) * (len(extent) - 1 - dim))
    return loudness


def scatter_about(key, shape, spread, bound, shards=(), kind=jnp.bfloat16):
    gain = steps_of(key, shape, shards, -0.22, 0.18) if shards else 1.0
    result = jax.random.normal(key, shape, jnp.float32) * spread * gain
    return jnp.minimum(jnp.maximum(result, -bound), bound).astype(kind)


def setup_inputs(seed: int = 0, part: int = 0) -> dict:
    arg_keys = jax.random.split(jax.random.key(seed), 12)
    own_keys = jax.random.split(jax.random.fold_in(arg_keys[11], part), 12)
    user_emb = draw_user_emb(jax.random.fold_in(jax.random.fold_in(arg_keys[11], part), 71), part)
    user_gate = draw_user_gate(jax.random.fold_in(jax.random.fold_in(arg_keys[11], part), 71), part)
    item_table = draw_item_table(jax.random.fold_in(jax.random.fold_in(arg_keys[11], part), 71), part)
    item_gate = scatter_about(own_keys[3], (NI, G), 1.0, 6.0, ((0, 16),))
    cand_ids = draw_cand_ids(jax.random.fold_in(jax.random.fold_in(arg_keys[11], part), 71), part)
    positives = touch_ends(jax.random.randint(own_keys[5], (ROUNDS, USERS), 0, NC), jax.random.fold_in(own_keys[5], 1), 0, NC - 1).astype(jnp.int32)
    loss_weight = jnp.clip(jnp.exp(jax.random.uniform(own_keys[6], (ROUNDS, USERS), jnp.float32, math.log(1.0), math.log(8.0))), 1.0, 8.0)
    w_in = scatter_about(arg_keys[7], (G, H), G ** -0.5, 0.75, (), jnp.float32)
    b_in = scatter_about(arg_keys[8], (H,), 1.0, 4.0, (), jnp.float32)
    w_out = scatter_about(arg_keys[9], (H, K), 0.3, 1.5, (), jnp.float32)
    b_out = scatter_about(arg_keys[10], (K,), 1.0, 4.0, (), jnp.float32)
    return {"user_emb": user_emb, "user_gate": user_gate, "item_table": item_table, "item_gate": item_gate, "cand_ids": cand_ids, "positives": positives, "loss_weight": loss_weight, "w_in": w_in, "b_in": b_in, "w_out": w_out, "b_out": b_out}


def forward(users, ugate_rows, items, igate_rows, w_in, b_in, w_out, b_out):
    count_u = users.shape[0]
    count_i = items.shape[0]
    comps = w_out.shape[1]
    depth = users.shape[1] // comps
    left = users.reshape(count_u, comps, depth).astype(jnp.float32)
    right = items.reshape(count_i, comps, depth).astype(jnp.float32)
    component = jnp.einsum('ukd,ikd->kui', left, right) * (1.0 / math.sqrt(depth))
    user_act = jnp.dot(ugate_rows.astype(jnp.float32), w_in, precision=lax.Precision.HIGHEST)
    item_act = jnp.dot(igate_rows.astype(jnp.float32), w_in, precision=lax.Precision.HIGHEST)
    preact = user_act[:, None, :] + item_act[None, :, :] + b_in
    hidden = jax.nn.silu(preact)
    gate_logit = jnp.einsum('uih,hk->kui', hidden, w_out, precision=lax.Precision.HIGHEST) + b_out[:, None, None]
    gates = jax.nn.softmax(gate_logit, axis=0)
    score = lax.optimization_barrier(jnp.sum(gates * component, 0))
    return (component, gates, score, preact)

def backward(users, items, w_in, w_out, component, gates, score, preact, top, total, pos_local, weight):
    count_u = users.shape[0]
    count_i = items.shape[0]
    comps = w_out.shape[1]
    depth = users.shape[1] // comps
    left = users.reshape(count_u, comps, depth).astype(jnp.float32)
    right = items.reshape(count_i, comps, depth).astype(jnp.float32)
    likely = jnp.exp(score - top[:, None]) / total[:, None]
    target = (jnp.arange(count_i, dtype=jnp.int32)[None, :] == pos_local[:, None]).astype(jnp.float32)
    score_grad = weight[:, None] * (likely - target)
    comp_grad = (score_grad[None] * gates).astype(jnp.bfloat16)
    comp_grad = lax.optimization_barrier(comp_grad).astype(jnp.float32)
    gate_grad = score_grad[None] * gates * (component - score[None])
    hidden_grad = jnp.einsum('kui,hk->uih', gate_grad, w_out, precision=lax.Precision.HIGHEST)
    sigma = jax.nn.sigmoid(preact)
    preact_grad = hidden_grad * sigma * (1.0 + preact * (1.0 - sigma))
    user_gate_part = jnp.dot(lax.optimization_barrier(jnp.sum(preact_grad, 1)), w_in.T, precision=lax.Precision.HIGHEST)
    item_gate_part = jnp.dot(lax.optimization_barrier(jnp.sum(preact_grad, 0)), w_in.T, precision=lax.Precision.HIGHEST)
    scale = 1.0 / math.sqrt(depth)
    user_part = (jnp.einsum('kui,ikd->ukd', comp_grad, right) * scale).reshape(count_u, comps * depth)
    item_part = (jnp.einsum('kui,ukd->ikd', comp_grad, left) * scale).reshape(count_i, comps * depth)
    return (user_part, user_gate_part, item_part, item_gate_part)

def reference(user_emb, user_gate, item_table, item_gate, cand_ids, positives, loss_weight, w_in, b_in, w_out, b_out):
    blocks = NC // IT_DEV
    table_grad = jnp.zeros(item_table.shape, jnp.float32)
    gate_table_grad = jnp.zeros(item_gate.shape, jnp.float32)
    user_grads = []
    gate_grads = []
    for turn in range(ROUNDS):
        users = user_emb[turn]
        ugate_rows = user_gate[turn]
        id_blocks = cand_ids[turn].reshape(blocks, IT_DEV)

        def score_block(rows):
            return forward(users, ugate_rows, item_table[rows], item_gate[rows], w_in, b_in, w_out, b_out)[2]
        scores = lax.map(score_block, id_blocks)
        top = lax.optimization_barrier(jnp.max(scores, axis=(0, 2)))
        total = lax.optimization_barrier(jnp.sum(jnp.exp(scores - top[None, :, None]), axis=(0, 2)))

        def grad_block(carry, inputs):
            rows, block_no = inputs
            items = item_table[rows]
            component, gates, score, preact = forward(users, ugate_rows, items, item_gate[rows], w_in, b_in, w_out, b_out)
            pos_local = positives[turn] - block_no * IT_DEV
            user_part, user_gate_part, item_part, item_gate_part = backward(users, items, w_in, w_out, component, gates, score, preact, top, total, pos_local, loss_weight[turn])
            return ((carry[0] + user_part, carry[1] + user_gate_part), (item_part, item_gate_part))
        start = (jnp.zeros((USERS, E), jnp.float32), jnp.zeros((USERS, G), jnp.float32))
        sums, parts = lax.scan(grad_block, start, (id_blocks, jnp.arange(blocks, dtype=jnp.int32)))
        user_grads.append(sums[0])
        gate_grads.append(sums[1])
        table_grad = table_grad.at[cand_ids[turn]].add(parts[0].reshape(NC, E))
        gate_table_grad = gate_table_grad.at[cand_ids[turn]].add(parts[1].reshape(NC, G))
    return (jnp.stack(user_grads), jnp.stack(gate_grads), table_grad, gate_table_grad)
```

```python
import functools
import math

import jax
import jax.numpy as jnp
from jax import lax
from jax.experimental import pallas as pl
from jax.experimental.pallas import tpu as pltpu
from jax.sharding import PartitionSpec as P

MESH = pl.DeviceIdType.MESH
F32 = jnp.float32
BF16 = jnp.bfloat16


def mm(a, b):
    return jnp.dot(a, b, preferred_element_type=F32)


def mm_nt(a, b):
    return lax.dot_general(a, b, (((1,), (1,)), ((), ())), preferred_element_type=F32)


def split(x):
    hi = x.astype(BF16)
    return hi, (x - hi.astype(F32)).astype(BF16)


def iota(shape, dim):
    return lax.broadcasted_iota(jnp.int32, shape, dim)


def to_col(row, rows):
    lanes = row.shape[1]
    keep = iota((rows, lanes), 0) == iota((rows, lanes), 1)
    return jnp.sum(jnp.where(keep, jnp.broadcast_to(row, (rows, lanes)), 0.0), 1, keepdims=True)


def to_row(col, lanes):
    rows = col.shape[0]
    keep = iota((rows, lanes), 0) == iota((rows, lanes), 1)
    return jnp.sum(jnp.where(keep, jnp.broadcast_to(col, (rows, lanes)), 0.0), 0, keepdims=True)


def kernel(
    n,
    dims,
    x_ref,
    tab_ref,
    ig_ref,
    ids_ref,
    pos_ref,
    lw_ref,
    win_ref,
    bin_ref,
    wout_ref,
    bout_ref,
    zo_ref,
    ugo_ref,
    tg_ref,
    gt_ref,
    ru,
    ubig,
    vals,
    iact,
    uact,
    comp_s,
    gate_s,
    score_s,
    st_out,
    st_in,
    ggt,
    cgt,
    si,
    up,
    us,
    zs,
    rz,
    ugs,
    rug,
    u_ss,
    u_rs,
    s_ss,
    s_rs,
    z_ss,
    z_rs,
    g_ss,
    g_rs,
):
    R, NU, UL, C, T, K, E, G, H = dims
    D = E // K
    HALF = E // 2
    scale = 1.0 / math.sqrt(D)
    me = lax.axis_index("items")

    def each_peer(make, act):
        def step(d, carry):
            act(make(d, lax.rem(me + d, n)))
            return carry

        lax.fori_loop(1, n, step, 0)

    def users_copy(d, peer):
        return pltpu.make_async_remote_copy(
            x_ref, ru.at[me], u_ss.at[d], u_rs.at[d], device_id={"items": peer}, device_id_type=MESH
        )

    def stats_copy(r):
        return lambda d, peer: pltpu.make_async_remote_copy(
            st_out.at[r],
            st_in.at[r, me],
            s_ss.at[r, d],
            s_rs.at[r, d],
            device_id={"items": peer},
            device_id_type=MESH,
        )

    def grads_copy(r):
        return lambda d, peer: pltpu.make_async_remote_copy(
            zs.at[r, peer],
            rz.at[r, me],
            z_ss.at[r, d],
            z_rs.at[r, d],
            device_id={"items": peer},
            device_id_type=MESH,
        )

    def gates_copy(d, peer):
        return pltpu.make_async_remote_copy(
            ugs.at[peer], rug.at[me], g_ss.at[d], g_rs.at[d], device_id={"items": peer}, device_id_type=MESH
        )

    def start(c):
        c.start()

    def wait_recv(c):
        c.wait_recv()

    def wait_send(c):
        c.wait_send()

    barrier = pltpu.get_barrier_semaphore()

    def greet(d, carry):
        pl.semaphore_signal(barrier, inc=1, device_id={"items": lax.rem(me + d, n)}, device_id_type=MESH)
        return carry

    lax.fori_loop(1, n, greet, 0)
    pl.semaphore_wait(barrier, n - 1)
    each_peer(users_copy, start)
    ru[me] = x_ref[...]

    w_in = win_ref[...]
    wi_hi, wi_lo = split(w_in)

    def onehot_cols(r):
        row = ids_ref[pl.ds(r, 1), :] - me * T
        return (iota((T, C), 0) == jnp.broadcast_to(row, (T, C))).astype(F32).astype(BF16)

    for r in range(R):
        row = (ids_ref[pl.ds(r, 1), :] - me * T).astype(F32)
        col = to_col(row, C).astype(jnp.int32)
        pick = (iota((C, T), 1) == jnp.broadcast_to(col, (C, T))).astype(F32).astype(BF16)
        vals[r] = mm(pick, tab_ref[...]).astype(BF16)
        q = mm(pick, ig_ref[...]).astype(BF16)
        iact[r] = 0.5 * (mm(q, wi_hi) + mm(q, wi_lo))

    each_peer(users_copy, wait_recv)

    packed = ru[...].reshape(n * 16, HALF + 128)
    rows = iota((R * NU, n * 16), 0)
    cols = iota((R * NU, n * 16), 1)
    turn, user = rows // NU, rows % NU
    where_to = (user // UL) * 16 + turn * UL + user % UL
    first = mm((cols == where_to).astype(F32).astype(BF16), packed)
    second = mm((cols == where_to + 8).astype(F32).astype(BF16), packed[:, :HALF])
    ug = first[:, HALF : HALF + G].astype(BF16)
    uact[...] = 0.5 * (mm(ug, wi_hi) + mm(ug, wi_lo) + bin_ref[...])
    for r in range(R):
        for half, part in enumerate((first[:, :HALF], second)):
            rows_r = part[r * NU : (r + 1) * NU]
            wide = jnp.broadcast_to(rows_r[:, None, :], (NU, K, HALF))
            mine = iota((NU, K, HALF), 1) == (iota((NU, K, HALF), 2) + half * HALF) // D
            ubig[r, :, half * HALF : (half + 1) * HALF] = (
                jnp.where(mine, wide, 0.0).reshape(NU * K, HALF).astype(BF16)
            )

    w_out = wout_ref[...]
    wo_hi = w_out.astype(BF16).astype(F32)
    wo_lo = w_out - wo_hi
    logit_w = jnp.concatenate(
        [jnp.concatenate([wo_hi, wo_hi], 1), jnp.concatenate([wo_lo, wo_lo], 1)], 0
    ).astype(BF16)
    b_col = to_col(bout_ref[...], K)

    STEP = 4
    for r in range(R):

        def fwd(i, carry, r=r):
            for s in range(STEP):
                u = i * STEP + s
                y = iact[r] + uact[pl.ds(r * NU + u, 1), :]
                t = jnp.tanh(y)
                h = y + y * t
                hi, lo = split(h)
                lg = mm_nt(logit_w, jnp.concatenate([hi, lo], 1))
                gate_s[r, pl.ds(pl.multiple_of(u * K, K), K), :] = lg[:K] + lg[K:] + b_col
            return carry

        lax.fori_loop(0, NU // STEP, fwd, 0)
        comp = (mm_nt(ubig[r], vals[r]) * scale).reshape(NU, K, C)
        lg = gate_s[r].reshape(NU, K, C)
        p = jnp.exp(lg - jnp.max(lg, 1, keepdims=True))
        gates = p / jnp.sum(p, 1, keepdims=True)
        score = jnp.sum(gates * comp, 1)
        comp_s[r] = comp.reshape(NU * K, C)
        gate_s[r] = gates.reshape(NU * K, C)
        score_s[r] = score
        ltop = jnp.max(score, 1, keepdims=True)
        ltot = jnp.sum(jnp.exp(score - ltop), 1, keepdims=True)
        st = jnp.where(iota((8, 128), 0) == 0, to_row(ltop, 128), to_row(ltot, 128))
        st_out[r] = st
        st_in[r, me] = st
        each_peer(stats_copy(r), start)

    whid = jnp.concatenate([wo_hi, wo_hi, wo_lo, wo_lo], 0) * 0.5
    whid = jnp.concatenate([whid] * 4, 0)
    whid = jnp.concatenate([whid] * 4, 1)
    keep = iota((16 * K, 4 * H), 0) // (4 * K) == iota((16 * K, 4 * H), 1) // H
    whid = jnp.where(keep, whid, 0.0).astype(BF16)
    eye = (iota((C, C), 0) == iota((C, C), 1)).astype(F32).astype(BF16)
    CH = 64
    gt_total = jnp.zeros((T, G), F32)
    for r in range(R):
        each_peer(stats_copy(r), wait_recv)
        st = st_in[r]
        tops, tots = st[:, 0, :], st[:, 1, :]
        top = jnp.max(tops, 0, keepdims=True)
        tot = jnp.sum(tots * jnp.exp(tops - top), 0, keepdims=True)
        top_c = to_col(top, NU)
        tot_c = to_col(tot, NU)
        w_c = to_col(lw_ref[pl.ds(r, 1), :], NU)
        pos_c = to_col((pos_ref[pl.ds(r, 1), :] - me * C).astype(F32), NU).astype(jnp.int32)
        score = score_s[r]
        hit = (iota((NU, C), 1) == pos_c).astype(F32)
        sg = w_c * (jnp.exp(score - top_c) / tot_c - hit)
        cg = sg[:, None, :] * gate_s[r].reshape(NU, K, C)
        gg = cg * (comp_s[r].reshape(NU, K, C) - score[:, None, :])
        cgb = cg.reshape(NU * K, C).astype(BF16)
        g_hi = gg.astype(BF16).astype(F32)
        g_lo = gg - g_hi
        g4 = jnp.concatenate([g_hi, g_lo, g_hi, g_lo], 1).reshape(NU * 4 * K, C).astype(BF16)
        ggt[...] = mm_nt(eye, g4).astype(BF16)

        wide = mm(cgb, vals[r])
        kk = iota((NU * K, D), 0) % K
        z = jnp.zeros((NU * K, D), F32)
        for k in range(K):
            z = jnp.where(kk == k, wide[:, k * D : (k + 1) * D], z)
        zb = (z * scale).astype(BF16).reshape(n, UL * K, D)
        zs[r] = zb
        rz[r, me] = zs[r, me]
        each_peer(grads_copy(r), start)

        hot = onehot_cols(r)
        cgt[r] = mm_nt(hot, cgb).astype(BF16)

        si[...] = jnp.zeros_like(si)

        def bwd(i, carry, r=r):
            sums = [jnp.zeros((8, H), F32) for _ in range(4)]
            lanes = pl.ds(pl.multiple_of(i * 128, 128), 128)
            for c in range(C // CH):
                at = pl.ds(c * CH, CH)
                hg = mm(ggt[at, lanes], whid)
                total = None
                for s in range(4):
                    y = iact[r, at, :] + uact[pl.ds(r * NU + i * 4 + s, 1), :]
                    t = jnp.tanh(y)
                    h = y + y * t
                    d2 = (1.0 + t) + h * (1.0 - t)
                    pg = hg[:, s * H : (s + 1) * H] * d2
                    sums[s] = sums[s] + jnp.sum(pg.reshape(CH // 8, 8, H), 0)
                    total = pg if total is None else total + pg
                si[at, :] = si[at, :] + total
            for s in range(4):
                up[i * 4 + s] = sums[s]
            return carry

        lax.fori_loop(0, NU // 4, bwd, 0)
        us[pl.ds(r * NU, NU), :] = jnp.sum(up[...], 1)
        s_hi, s_lo = split(si[...])
        ip = mm_nt(s_hi, wi_hi) + mm_nt(s_lo, wi_hi) + mm_nt(s_hi, wi_lo)
        p_hi, p_lo = split(ip)
        gt_total = gt_total + mm(hot, p_hi) + mm(hot, p_lo)

    u_hi, u_lo = split(us[...])
    rows = iota((n * 8, R * NU), 0)
    cols = iota((n * 8, R * NU), 1)
    owner, slot = rows // 8, rows % 8
    perm = (cols == (slot // UL) * NU + owner * UL + slot % UL).astype(F32).astype(BF16)
    o_hi, o_lo = mm(perm, u_hi).astype(BF16), mm(perm, u_lo).astype(BF16)
    w2_hi = jnp.concatenate([wi_hi.astype(F32), jnp.zeros((128 - G, H), F32)], 0).astype(BF16)
    w2_lo = jnp.concatenate([wi_lo.astype(F32), jnp.zeros((128 - G, H), F32)], 0).astype(BF16)
    ugp = mm_nt(o_hi, w2_hi) + mm_nt(o_lo, w2_hi) + mm_nt(o_hi, w2_lo)
    ugs[...] = ugp.reshape(n, 8, 128)
    rug[me] = ugs[me]
    each_peer(gates_copy, start)

    gt_ref[...] = gt_total
    tg = None
    for r in range(R):
        part = mm(cgt[r], ubig[r])
        tg = part if tg is None else tg + part
    tg_ref[...] = tg * scale

    for r in range(R):
        each_peer(grads_copy(r), wait_recv)
        zo_ref[r] = jnp.sum(rz[r].astype(F32), 0)
    each_peer(gates_copy, wait_recv)
    ugo_ref[...] = jnp.sum(rug[...], 0)
    each_peer(users_copy, wait_send)
    for r in range(R):
        each_peer(stats_copy(r), wait_send)
        each_peer(grads_copy(r), wait_send)
    each_peer(gates_copy, wait_send)


def body(
    n,
    user_emb,
    user_gate,
    item_table,
    item_gate,
    cand_ids,
    positives,
    loss_weight,
    w_in,
    b_in,
    w_out,
    b_out,
):
    R, UL, E = user_emb.shape
    G = user_gate.shape[2]
    NU = positives.shape[1]
    C = cand_ids.shape[1]
    T = item_table.shape[0]
    H, K = w_out.shape
    D = E // K
    assert R * UL == 8 and UL * K == 16 and NU == UL * n
    flat = user_emb.reshape(R * UL, E)
    low = jnp.concatenate([flat[:, : E // 2], jnp.pad(user_gate.reshape(R * UL, G), ((0, 0), (0, 128 - G)))], 1)
    high = jnp.pad(flat[:, E // 2 :], ((0, 0), (0, 128)))
    x = jnp.concatenate([low, high], 0)
    dims = (R, NU, UL, C, T, K, E, G, H)
    vm = pl.BlockSpec(memory_space=pltpu.VMEM)
    dma = pltpu.SemaphoreType.DMA
    z, ug, tg, gt = pl.pallas_call(
        functools.partial(kernel, n, dims),
        out_shape=(
            jax.ShapeDtypeStruct((R, UL * K, D), F32),
            jax.ShapeDtypeStruct((R * UL, 128), F32),
            jax.ShapeDtypeStruct((T, E), F32),
            jax.ShapeDtypeStruct((T, G), F32),
        ),
        in_specs=[vm] * 10,
        out_specs=(vm,) * 4,
        scratch_shapes=[
            pltpu.VMEM((n, 16, E // 2 + 128), BF16),
            pltpu.VMEM((R, NU * K, E), BF16),
            pltpu.VMEM((R, C, E), BF16),
            pltpu.VMEM((R, C, H), F32),
            pltpu.VMEM((R * NU, H), F32),
            pltpu.VMEM((R, NU * K, C), F32),
            pltpu.VMEM((R, NU * K, C), F32),
            pltpu.VMEM((R, NU, C), F32),
            pltpu.VMEM((R, 8, 128), F32),
            pltpu.VMEM((R, n, 8, 128), F32),
            pltpu.VMEM((C, NU * 4 * K), BF16),
            pltpu.VMEM((R, T, NU * K), BF16),
            pltpu.VMEM((C, H), F32),
            pltpu.VMEM((NU, 8, H), F32),
            pltpu.VMEM((R * NU, H), F32),
            pltpu.VMEM((R, n, UL * K, D), BF16),
            pltpu.VMEM((R, n, UL * K, D), BF16),
            pltpu.VMEM((n, 8, 128), F32),
            pltpu.VMEM((n, 8, 128), F32),
            dma((n,)),
            dma((n,)),
            dma((R, n)),
            dma((R, n)),
            dma((R, n)),
            dma((R, n)),
            dma((n,)),
            dma((n,)),
        ],
        compiler_params=pltpu.CompilerParams(
            collective_id=0, has_side_effects=True, vmem_limit_bytes=60 * 1024 * 1024
        ),
    )(
        x,
        item_table,
        item_gate,
        cand_ids,
        positives,
        loss_weight,
        w_in,
        b_in.reshape(1, H),
        w_out.T,
        b_out.reshape(1, K),
    )
    return (
        z.reshape(R, UL, E),
        ug[:, :G].reshape(R, UL, G),
        tg,
        gt,
    )


def solution(mesh):
    return jax.shard_map(
        functools.partial(body, mesh.shape["items"]),
        mesh=mesh,
        in_specs=(
            P(None, ("parts", "items"), None),
            P(None, ("parts", "items"), None),
            P(("parts", "items"), None),
            P(("parts", "items"), None),
            P(None, ("parts", "items")),
            P(None, "parts"),
            P(None, "parts"),
            P(),
            P(),
            P(),
            P(),
        ),
        out_specs=(
            P(None, ("parts", "items"), None),
            P(None, ("parts", "items"), None),
            P(("parts", "items"), None),
            P(("parts", "items"), None),
        ),
        check_vma=False,
    )
```

```python
import functools
import math

import jax
import jax.numpy as jnp
from jax import lax
from jax.experimental import pallas as pl
from jax.experimental.pallas import tpu as pltpu
from jax.sharding import PartitionSpec as P

MESH = pl.DeviceIdType.MESH
F32 = jnp.float32
BF16 = jnp.bfloat16


def mm(a, b):
    return jnp.dot(a, b, preferred_element_type=F32)


def mm_nt(a, b):
    return lax.dot_general(a, b, (((1,), (1,)), ((), ())), preferred_element_type=F32)


def split(x):
    hi = x.astype(BF16)
    return hi, (x - hi.astype(F32)).astype(BF16)


def iota(shape, dim):
    return lax.broadcasted_iota(jnp.int32, shape, dim)


def to_col(row, rows):
    lanes = row.shape[1]
    keep = iota((rows, lanes), 0) == iota((rows, lanes), 1)
    return jnp.sum(jnp.where(keep, jnp.broadcast_to(row, (rows, lanes)), 0.0), 1, keepdims=True)


def to_row(col, lanes):
    rows = col.shape[0]
    keep = iota((rows, lanes), 0) == iota((rows, lanes), 1)
    return jnp.sum(jnp.where(keep, jnp.broadcast_to(col, (rows, lanes)), 0.0), 0, keepdims=True)


def kernel(
    n,
    dims,
    x_ref,
    tab_ref,
    ig_ref,
    ids_ref,
    pos_ref,
    lw_ref,
    win_ref,
    bin_ref,
    wout_ref,
    bout_ref,
    zo_ref,
    ugo_ref,
    tg_ref,
    gt_ref,
    ru,
    ubig,
    vals,
    iact,
    uact,
    comp_s,
    gate_s,
    score_s,
    st_out,
    st_in,
    ggt,
    cgt,
    si,
    up,
    us,
    zs,
    rz,
    ugs,
    rug,
    u_ss,
    u_rs,
    s_ss,
    s_rs,
    z_ss,
    z_rs,
    g_ss,
    g_rs,
):
    R, NU, UL, C, T, K, E, G, H = dims
    D = E // K
    HALF = E // 2
    scale = 1.0 / math.sqrt(D)
    me = lax.axis_index("items")

    def around(d):
        peer = me + d
        return jnp.where(peer >= n, peer - n, peer)

    def send(src, dst, ss, rs):
        def step(d, carry):
            peer = around(d)
            pltpu.make_async_remote_copy(
                src(peer), dst, ss, rs, device_id={"items": peer}, device_id_type=MESH
            ).start()
            return carry

        lax.fori_loop(1, n, step, 0)

    def await_all(blocks, sem):
        pltpu.make_async_copy(blocks, blocks, sem).wait()

    others = pl.ds(0, n - 1)
    groups = ((0, R - 1), (R - 1, 1)) if R > 1 else ((0, R),)

    barrier = pltpu.get_barrier_semaphore()

    def greet(d, carry):
        pl.semaphore_signal(barrier, inc=1, device_id={"items": around(d)}, device_id_type=MESH)
        return carry

    lax.fori_loop(1, n, greet, 0)
    pl.semaphore_wait(barrier, n - 1)
    send(lambda peer: x_ref, ru.at[me], u_ss, u_rs)
    ru[me] = x_ref[...]

    w_in = win_ref[...]
    wi_hi, wi_lo = split(w_in)

    def onehot_cols(r):
        row = ids_ref[pl.ds(r, 1), :] - me * T
        return (iota((T, C), 0) == jnp.broadcast_to(row, (T, C))).astype(F32).astype(BF16)

    for r in range(R):
        row = (ids_ref[pl.ds(r, 1), :] - me * T).astype(F32)
        col = to_col(row, C).astype(jnp.int32)
        pick = (iota((C, T), 1) == jnp.broadcast_to(col, (C, T))).astype(F32).astype(BF16)
        vals[r] = mm(pick, tab_ref[...]).astype(BF16)
        q = mm_nt(pick, ig_ref[...]).astype(BF16)
        iact[r] = 0.5 * (mm(q, wi_hi) + mm(q, wi_lo))

    await_all(ru.at[others], u_rs)

    packed = ru[...].reshape(n * 16, HALF + 128)
    rows = iota((R * NU, n * 16), 0)
    cols = iota((R * NU, n * 16), 1)
    turn, user = rows // NU, rows % NU
    where_to = (user // UL) * 16 + turn * UL + user % UL
    first = mm((cols == where_to).astype(F32).astype(BF16), packed)
    second = mm((cols == where_to + 8).astype(F32).astype(BF16), packed[:, :HALF])
    ug = first[:, HALF : HALF + G].astype(BF16)
    uact[...] = 0.5 * (mm(ug, wi_hi) + mm(ug, wi_lo) + bin_ref[...])
    for r in range(R):
        for half, part in enumerate((first[:, :HALF], second)):
            rows_r = part[r * NU : (r + 1) * NU]
            wide = jnp.broadcast_to(rows_r[:, None, :], (NU, K, HALF))
            mine = iota((NU, K, HALF), 1) == (iota((NU, K, HALF), 2) + half * HALF) // D
            ubig[r, :, half * HALF : (half + 1) * HALF] = (
                jnp.where(mine, wide, 0.0).reshape(NU * K, HALF).astype(BF16)
            )

    w_out = wout_ref[...]
    wo_hi = w_out.astype(BF16).astype(F32)
    wo_lo = w_out - wo_hi
    logit_w = jnp.concatenate(
        [jnp.concatenate([wo_hi, wo_hi], 1), jnp.concatenate([wo_lo, wo_lo], 1)], 0
    ).astype(BF16)
    b_col = to_col(bout_ref[...], K)

    STEP = 4
    for r in range(R):

        def fwd(i, carry, r=r):
            for s in range(STEP):
                u = i * STEP + s
                y = iact[r] + uact[pl.ds(r * NU + u, 1), :]
                t = jnp.tanh(y)
                h = y + y * t
                hi, lo = split(h)
                lg = mm_nt(logit_w, jnp.concatenate([hi, lo], 1))
                gate_s[r, pl.ds(pl.multiple_of(u * K, K), K), :] = lg[:K] + lg[K:] + b_col
            return carry

        lax.fori_loop(0, NU // STEP, fwd, 0)
        comp = (mm_nt(ubig[r], vals[r]) * scale).reshape(NU, K, C)
        lg = gate_s[r].reshape(NU, K, C)
        p = jnp.exp(lg - jnp.max(lg, 1, keepdims=True))
        gates = p / jnp.sum(p, 1, keepdims=True)
        score = jnp.sum(gates * comp, 1)
        comp_s[r] = comp.reshape(NU * K, C)
        gate_s[r] = gates.reshape(NU * K, C)
        score_s[r] = score
        ltop = jnp.max(score, 1, keepdims=True)
        ltot = jnp.sum(jnp.exp(score - ltop), 1, keepdims=True)
        st = jnp.where(iota((8, 128), 0) == 0, to_row(ltop, 128), to_row(ltot, 128))
        st_out[r] = st
        st_in[me, r] = st
        for g, (r0, cnt) in enumerate(groups):
            if r == r0 + cnt - 1:
                at = pl.ds(r0, cnt)
                send(lambda peer: st_out.at[at], st_in.at[me, at], s_ss.at[g], s_rs.at[g])

    whid = jnp.concatenate([wo_hi, wo_hi, wo_lo, wo_lo], 0) * 0.5
    whid = jnp.concatenate([whid] * 4, 0)
    whid = jnp.concatenate([whid] * 4, 1)
    keep = iota((16 * K, 4 * H), 0) // (4 * K) == iota((16 * K, 4 * H), 1) // H
    whid = jnp.where(keep, whid, 0.0).astype(BF16)
    eye = (iota((C, C), 0) == iota((C, C), 1)).astype(F32).astype(BF16)
    CH = 64
    gt_total = jnp.zeros((G, T), F32)
    for r in range(R):
        for g, (r0, cnt) in enumerate(groups):
            if r == r0:
                await_all(st_in.at[others, pl.ds(r0, cnt)], s_rs.at[g])
        st = st_in[:, r]
        tops, tots = st[:, 0, :], st[:, 1, :]
        top = jnp.max(tops, 0, keepdims=True)
        tot = jnp.sum(tots * jnp.exp(tops - top), 0, keepdims=True)
        top_c = to_col(top, NU)
        tot_c = to_col(tot, NU)
        w_c = to_col(lw_ref[pl.ds(r, 1), :], NU)
        pos_c = to_col((pos_ref[pl.ds(r, 1), :] - me * C).astype(F32), NU).astype(jnp.int32)
        score = score_s[r]
        hit = (iota((NU, C), 1) == pos_c).astype(F32)
        sg = w_c * (jnp.exp(score - top_c) / tot_c - hit)
        cg = sg[:, None, :] * gate_s[r].reshape(NU, K, C)
        gg = cg * (comp_s[r].reshape(NU, K, C) - score[:, None, :])
        cgb = cg.reshape(NU * K, C).astype(BF16)
        g_hi = gg.astype(BF16).astype(F32)
        g_lo = gg - g_hi
        g4 = jnp.concatenate([g_hi, g_lo, g_hi, g_lo], 1).reshape(NU * 4 * K, C).astype(BF16)
        ggt[...] = mm_nt(eye, g4).astype(BF16)

        wide = mm(cgb, vals[r])
        kk = iota((NU * K, D), 0) % K
        z = jnp.zeros((NU * K, D), F32)
        for k in range(K):
            z = jnp.where(kk == k, wide[:, k * D : (k + 1) * D], z)
        zb = (z * scale).astype(BF16).reshape(n, UL * K, D)
        zs[:, r] = zb
        rz[me, r] = zs[me, r]
        for g, (r0, cnt) in enumerate(groups):
            if r == r0 + cnt - 1:
                at = pl.ds(r0, cnt)
                send(lambda peer: zs.at[peer, at], rz.at[me, at], z_ss.at[g], z_rs.at[g])

        hot = onehot_cols(r)
        cgt[r] = mm_nt(hot, cgb).astype(BF16)

        si[...] = jnp.zeros_like(si)

        def bwd(i, carry, r=r):
            sums = [jnp.zeros((8, H), F32) for _ in range(4)]
            lanes = pl.ds(pl.multiple_of(i * 128, 128), 128)
            for c in range(C // CH):
                at = pl.ds(c * CH, CH)
                hg = mm(ggt[at, lanes], whid)
                total = None
                for s in range(4):
                    y = iact[r, at, :] + uact[pl.ds(r * NU + i * 4 + s, 1), :]
                    t = jnp.tanh(y)
                    h = y + y * t
                    d2 = (1.0 + t) + h * (1.0 - t)
                    pg = hg[:, s * H : (s + 1) * H] * d2
                    sums[s] = sums[s] + jnp.sum(pg.reshape(CH // 8, 8, H), 0)
                    total = pg if total is None else total + pg
                si[at, :] = si[at, :] + total
            for s in range(4):
                up[i * 4 + s] = sums[s]
            return carry

        lax.fori_loop(0, NU // 4, bwd, 0)
        us[pl.ds(r * NU, NU), :] = jnp.sum(up[...], 1)
        s_hi, s_lo = split(si[...])
        ip = mm_nt(wi_hi, s_hi) + mm_nt(wi_hi, s_lo) + mm_nt(wi_lo, s_hi)
        p_hi, p_lo = split(ip)
        gt_total = gt_total + mm_nt(p_hi, hot) + mm_nt(p_lo, hot)

    u_hi, u_lo = split(us[...])
    rows = iota((n * 8, R * NU), 0)
    cols = iota((n * 8, R * NU), 1)
    owner, slot = rows // 8, rows % 8
    perm = (cols == (slot // UL) * NU + owner * UL + slot % UL).astype(F32).astype(BF16)
    o_hi, o_lo = mm(perm, u_hi).astype(BF16), mm(perm, u_lo).astype(BF16)
    w2_hi = jnp.concatenate([wi_hi.astype(F32), jnp.zeros((128 - G, H), F32)], 0).astype(BF16)
    w2_lo = jnp.concatenate([wi_lo.astype(F32), jnp.zeros((128 - G, H), F32)], 0).astype(BF16)
    ugp = mm_nt(o_hi, w2_hi) + mm_nt(o_lo, w2_hi) + mm_nt(o_hi, w2_lo)
    ugs[...] = ugp.reshape(n, 8, 128)
    rug[me] = ugs[me]
    send(lambda peer: ugs.at[peer], rug.at[me], g_ss, g_rs)

    gt_ref[...] = gt_total
    tg = None
    for r in range(R):
        part = mm(cgt[r], ubig[r])
        tg = part if tg is None else tg + part
    tg_ref[...] = tg * scale

    for g, (r0, cnt) in enumerate(groups):
        await_all(rz.at[others, pl.ds(r0, cnt)], z_rs.at[g])
        for r in range(r0, r0 + cnt):
            zo_ref[r] = jnp.sum(rz[:, r].astype(F32), 0)
    await_all(rug.at[others], g_rs)
    ugo_ref[...] = jnp.sum(rug[...], 0)
    await_all(ru.at[others], u_ss)
    for g, (r0, cnt) in enumerate(groups):
        await_all(st_in.at[others, pl.ds(r0, cnt)], s_ss.at[g])
        await_all(zs.at[others, pl.ds(r0, cnt)], z_ss.at[g])
    await_all(ugs.at[others], g_ss)


def body(
    n,
    user_emb,
    user_gate,
    item_table,
    item_gate,
    cand_ids,
    positives,
    loss_weight,
    w_in,
    b_in,
    w_out,
    b_out,
):
    R, UL, E = user_emb.shape
    G = user_gate.shape[2]
    NU = positives.shape[1]
    C = cand_ids.shape[1]
    T = item_table.shape[0]
    H, K = w_out.shape
    D = E // K
    assert R * UL == 8 and UL * K == 16 and NU == UL * n
    flat = user_emb.reshape(R * UL, E)
    low = jnp.concatenate([flat[:, : E // 2], jnp.pad(user_gate.reshape(R * UL, G), ((0, 0), (0, 128 - G)))], 1)
    high = jnp.pad(flat[:, E // 2 :], ((0, 0), (0, 128)))
    x = jnp.concatenate([low, high], 0)
    dims = (R, NU, UL, C, T, K, E, G, H)
    vm = pl.BlockSpec(memory_space=pltpu.VMEM)
    dma = pltpu.SemaphoreType.DMA
    z, ug, tg, gt = pl.pallas_call(
        functools.partial(kernel, n, dims),
        out_shape=(
            jax.ShapeDtypeStruct((R, UL * K, D), F32),
            jax.ShapeDtypeStruct((R * UL, 128), F32),
            jax.ShapeDtypeStruct((T, E), F32),
            jax.ShapeDtypeStruct((G, T), F32),
        ),
        in_specs=[vm] * 10,
        out_specs=(vm,) * 4,
        scratch_shapes=[
            pltpu.VMEM((n, 16, E // 2 + 128), BF16),
            pltpu.VMEM((R, NU * K, E), BF16),
            pltpu.VMEM((R, C, E), BF16),
            pltpu.VMEM((R, C, H), F32),
            pltpu.VMEM((R * NU, H), F32),
            pltpu.VMEM((R, NU * K, C), F32),
            pltpu.VMEM((R, NU * K, C), F32),
            pltpu.VMEM((R, NU, C), F32),
            pltpu.VMEM((R, 8, 128), F32),
            pltpu.VMEM((n, R, 8, 128), F32),
            pltpu.VMEM((C, NU * 4 * K), BF16),
            pltpu.VMEM((R, T, NU * K), BF16),
            pltpu.VMEM((C, H), F32),
            pltpu.VMEM((NU, 8, H), F32),
            pltpu.VMEM((R * NU, H), F32),
            pltpu.VMEM((n, R, UL * K, D), BF16),
            pltpu.VMEM((n, R, UL * K, D), BF16),
            pltpu.VMEM((n, 8, 128), F32),
            pltpu.VMEM((n, 8, 128), F32),
            dma,
            dma,
            dma((2,)),
            dma((2,)),
            dma((2,)),
            dma((2,)),
            dma,
            dma,
        ],
        compiler_params=pltpu.CompilerParams(
            collective_id=0, has_side_effects=True, vmem_limit_bytes=60 * 1024 * 1024
        ),
    )(
        x,
        item_table,
        item_gate.T,
        cand_ids,
        positives,
        loss_weight,
        w_in,
        b_in.reshape(1, H),
        w_out.T,
        b_out.reshape(1, K),
    )
    return (
        z.reshape(R, UL, E),
        ug[:, :G].reshape(R, UL, G),
        tg,
        gt.T,
    )


def solution(mesh):
    return jax.shard_map(
        functools.partial(body, mesh.shape["items"]),
        mesh=mesh,
        in_specs=(
            P(None, ("parts", "items"), None),
            P(None, ("parts", "items"), None),
            P(("parts", "items"), None),
            P(("parts", "items"), None),
            P(None, ("parts", "items")),
            P(None, "parts"),
            P(None, "parts"),
            P(),
            P(),
            P(),
            P(),
        ),
        out_specs=(
            P(None, ("parts", "items"), None),
            P(None, ("parts", "items"), None),
            P(("parts", "items"), None),
            P(("parts", "items"), None),
        ),
        check_vma=False,
    )
```

```python
import functools
import math

import jax
import jax.numpy as jnp
from jax import lax
from jax.experimental import pallas as pl
from jax.experimental.pallas import tpu as pltpu
from jax.sharding import PartitionSpec as P

MESH = pl.DeviceIdType.MESH
F32 = jnp.float32
BF16 = jnp.bfloat16


def mm(a, b):
    return jnp.dot(a, b, preferred_element_type=F32)


def mm_nt(a, b):
    return lax.dot_general(a, b, (((1,), (1,)), ((), ())), preferred_element_type=F32)


def split(x):
    hi = x.astype(BF16)
    return hi, (x - hi.astype(F32)).astype(BF16)


def iota(shape, dim):
    return lax.broadcasted_iota(jnp.int32, shape, dim)


def to_col(row, rows):
    lanes = row.shape[1]
    keep = iota((rows, lanes), 0) == iota((rows, lanes), 1)
    return jnp.sum(jnp.where(keep, jnp.broadcast_to(row, (rows, lanes)), 0.0), 1, keepdims=True)


def to_row(col, lanes):
    rows = col.shape[0]
    keep = iota((rows, lanes), 0) == iota((rows, lanes), 1)
    return jnp.sum(jnp.where(keep, jnp.broadcast_to(col, (rows, lanes)), 0.0), 0, keepdims=True)


def kernel(
    n,
    dims,
    x_ref,
    tab_ref,
    ig_ref,
    ids_ref,
    pos_ref,
    lw_ref,
    win_ref,
    bin_ref,
    wout_ref,
    bout_ref,
    zo_ref,
    ugo_ref,
    tg_ref,
    gt_ref,
    ru,
    ubig,
    vals,
    iact,
    uact,
    comp_s,
    gate_s,
    score_s,
    st_out,
    st_in,
    ggt,
    cgt,
    si,
    up,
    us,
    zs,
    rz,
    ugs,
    rug,
    u_ss,
    u_rs,
    s_ss,
    s_rs,
    z_ss,
    z_rs,
    g_ss,
    g_rs,
):
    R, NU, UL, C, T, K, E, G, H = dims
    D = E // K
    HALF = E // 2
    scale = 1.0 / math.sqrt(D)
    me = lax.axis_index("items")

    def around(d):
        peer = me + d
        return jnp.where(peer >= n, peer - n, peer)

    def send(src, dst, ss, rs):
        def step(d, carry):
            peer = around(d)
            pltpu.make_async_remote_copy(
                src(peer), dst, ss, rs, device_id={"items": peer}, device_id_type=MESH
            ).start()
            return carry

        lax.fori_loop(1, n, step, 0)

    def await_all(blocks, sem):
        pltpu.make_async_copy(blocks, blocks, sem).wait()

    others = pl.ds(0, n - 1)
    groups = ((0, R - 1), (R - 1, 1)) if R > 1 else ((0, R),)

    barrier = pltpu.get_barrier_semaphore()

    def greet(d, carry):
        pl.semaphore_signal(barrier, inc=1, device_id={"items": around(d)}, device_id_type=MESH)
        return carry

    lax.fori_loop(1, n, greet, 0)

    w_in = win_ref[...]
    wi_hi, wi_lo = split(w_in)

    def onehot_cols(r):
        row = ids_ref[pl.ds(r, 1), :] - me * T
        return (iota((T, C), 0) == jnp.broadcast_to(row, (T, C))).astype(F32).astype(BF16)

    for r in range(R):
        row = (ids_ref[pl.ds(r, 1), :] - me * T).astype(F32)
        col = to_col(row, C).astype(jnp.int32)
        pick = (iota((C, T), 1) == jnp.broadcast_to(col, (C, T))).astype(F32).astype(BF16)
        vals[r] = mm(pick, tab_ref[...]).astype(BF16)
        q = mm_nt(pick, ig_ref[...]).astype(BF16)
        iact[r] = 0.5 * (mm(q, wi_hi) + mm(q, wi_lo))
        if r == 0:
            pl.semaphore_wait(barrier, n - 1)
            send(lambda peer: x_ref, ru.at[me], u_ss, u_rs)
            ru[me] = x_ref[...]

    await_all(ru.at[others], u_rs)

    packed = ru[...].reshape(n * 16, HALF + 128)
    rows = iota((R * NU, n * 16), 0)
    cols = iota((R * NU, n * 16), 1)
    turn, user = rows // NU, rows % NU
    where_to = (user // UL) * 16 + turn * UL + user % UL
    first = mm((cols == where_to).astype(F32).astype(BF16), packed)
    second = mm((cols == where_to + 8).astype(F32).astype(BF16), packed[:, :HALF])
    ug = first[:, HALF : HALF + G].astype(BF16)
    uact[...] = 0.5 * (mm(ug, wi_hi) + mm(ug, wi_lo) + bin_ref[...])
    for r in range(R):
        for half, part in enumerate((first[:, :HALF], second)):
            rows_r = part[r * NU : (r + 1) * NU]
            wide = jnp.broadcast_to(rows_r[:, None, :], (NU, K, HALF))
            mine = iota((NU, K, HALF), 1) == (iota((NU, K, HALF), 2) + half * HALF) // D
            ubig[r, :, half * HALF : (half + 1) * HALF] = (
                jnp.where(mine, wide, 0.0).reshape(NU * K, HALF).astype(BF16)
            )

    w_out = wout_ref[...]
    wo_hi = w_out.astype(BF16).astype(F32)
    wo_lo = w_out - wo_hi
    logit_w = jnp.concatenate(
        [jnp.concatenate([wo_hi, wo_hi], 1), jnp.concatenate([wo_lo, wo_lo], 1)], 0
    ).astype(BF16)
    b_col = to_col(bout_ref[...], K)

    STEP = 4
    for r in range(R):

        def fwd(i, carry, r=r):
            for s in range(STEP):
                u = i * STEP + s
                y = iact[r] + uact[pl.ds(r * NU + u, 1), :]
                t = jnp.tanh(y)
                h = y + y * t
                hi, lo = split(h)
                lg = mm_nt(logit_w, jnp.concatenate([hi, lo], 1))
                gate_s[r, pl.ds(pl.multiple_of(u * K, K), K), :] = lg[:K] + lg[K:] + b_col
            return carry

        lax.fori_loop(0, NU // STEP, fwd, 0)
        comp = (mm_nt(ubig[r], vals[r]) * scale).reshape(NU, K, C)
        lg = gate_s[r].reshape(NU, K, C)
        p = jnp.exp(lg - jnp.max(lg, 1, keepdims=True))
        gates = p / jnp.sum(p, 1, keepdims=True)
        score = jnp.sum(gates * comp, 1)
        comp_s[r] = comp.reshape(NU * K, C)
        gate_s[r] = gates.reshape(NU * K, C)
        score_s[r] = score
        ltop = jnp.max(score, 1, keepdims=True)
        ltot = jnp.sum(jnp.exp(score - ltop), 1, keepdims=True)
        st = jnp.where(iota((8, 128), 0) == 0, to_row(ltop, 128), to_row(ltot, 128))
        st_out[r] = st
        st_in[me, r] = st
        for g, (r0, cnt) in enumerate(groups):
            if r == r0 + cnt - 1:
                at = pl.ds(r0, cnt)
                send(lambda peer: st_out.at[at], st_in.at[me, at], s_ss.at[g], s_rs.at[g])

    whid = jnp.concatenate([wo_hi, wo_hi, wo_lo, wo_lo], 0) * 0.5
    whid = jnp.concatenate([whid] * 4, 0)
    whid = jnp.concatenate([whid] * 4, 1)
    keep = iota((16 * K, 4 * H), 0) // (4 * K) == iota((16 * K, 4 * H), 1) // H
    whid = jnp.where(keep, whid, 0.0).astype(BF16)
    eye = (iota((C, C), 0) == iota((C, C), 1)).astype(F32).astype(BF16)
    CH = 64
    gt_total = jnp.zeros((G, T), F32)
    for r in range(R):
        for g, (r0, cnt) in enumerate(groups):
            if r == r0:
                await_all(st_in.at[others, pl.ds(r0, cnt)], s_rs.at[g])
        st = st_in[:, r]
        tops, tots = st[:, 0, :], st[:, 1, :]
        top = jnp.max(tops, 0, keepdims=True)
        tot = jnp.sum(tots * jnp.exp(tops - top), 0, keepdims=True)
        top_c = to_col(top, NU)
        tot_c = to_col(tot, NU)
        w_c = to_col(lw_ref[pl.ds(r, 1), :], NU)
        pos_c = to_col((pos_ref[pl.ds(r, 1), :] - me * C).astype(F32), NU).astype(jnp.int32)
        score = score_s[r]
        hit = (iota((NU, C), 1) == pos_c).astype(F32)
        sg = w_c * (jnp.exp(score - top_c) / tot_c - hit)
        cg = sg[:, None, :] * gate_s[r].reshape(NU, K, C)
        gg = cg * (comp_s[r].reshape(NU, K, C) - score[:, None, :])
        cgb = cg.reshape(NU * K, C).astype(BF16)
        g_hi = gg.astype(BF16).astype(F32)
        g_lo = gg - g_hi
        g4 = jnp.concatenate([g_hi, g_lo, g_hi, g_lo], 1).reshape(NU * 4 * K, C).astype(BF16)
        ggt[...] = mm_nt(eye, g4).astype(BF16)

        wide = mm(cgb, vals[r])
        kk = iota((NU * K, D), 0) % K
        z = jnp.zeros((NU * K, D), F32)
        for k in range(K):
            z = jnp.where(kk == k, wide[:, k * D : (k + 1) * D], z)
        zb = (z * scale).astype(BF16).reshape(n, UL * K, D)
        zs[:, r] = zb
        rz[me, r] = zs[me, r]
        for g, (r0, cnt) in enumerate(groups):
            if r == r0 + cnt - 1:
                at = pl.ds(r0, cnt)
                send(lambda peer: zs.at[peer, at], rz.at[me, at], z_ss.at[g], z_rs.at[g])

        hot = onehot_cols(r)
        cgt[:, r * NU * K : (r + 1) * NU * K] = mm_nt(hot, cgb).astype(BF16)

        si[...] = jnp.zeros_like(si)

        def bwd(i, carry, r=r):
            sums = [jnp.zeros((8, H), F32) for _ in range(4)]
            lanes = pl.ds(pl.multiple_of(i * 128, 128), 128)
            for c in range(C // CH):
                at = pl.ds(c * CH, CH)
                hg = mm(ggt[at, lanes], whid)
                total = None
                for s in range(4):
                    y = iact[r, at, :] + uact[pl.ds(r * NU + i * 4 + s, 1), :]
                    t = jnp.tanh(y)
                    h = y + y * t
                    d2 = (1.0 + t) + h * (1.0 - t)
                    pg = hg[:, s * H : (s + 1) * H] * d2
                    sums[s] = sums[s] + jnp.sum(pg.reshape(CH // 8, 8, H), 0)
                    total = pg if total is None else total + pg
                si[at, :] = si[at, :] + total
            for s in range(4):
                up[i * 4 + s] = sums[s]
            return carry

        lax.fori_loop(0, NU // 4, bwd, 0)
        us[pl.ds(r * NU, NU), :] = jnp.sum(up[...], 1)
        s_hi, s_lo = split(si[...])
        ip = mm_nt(wi_hi, s_hi) + mm_nt(wi_hi, s_lo) + mm_nt(wi_lo, s_hi)
        p_hi, p_lo = split(ip)
        gt_total = gt_total + mm_nt(p_hi, hot) + mm_nt(p_lo, hot)

    u_hi, u_lo = split(us[...])
    rows = iota((n * 8, R * NU), 0)
    cols = iota((n * 8, R * NU), 1)
    owner, slot = rows // 8, rows % 8
    perm = (cols == (slot // UL) * NU + owner * UL + slot % UL).astype(F32).astype(BF16)
    o_hi, o_lo = mm(perm, u_hi).astype(BF16), mm(perm, u_lo).astype(BF16)
    w2_hi = jnp.concatenate([wi_hi.astype(F32), jnp.zeros((128 - G, H), F32)], 0).astype(BF16)
    w2_lo = jnp.concatenate([wi_lo.astype(F32), jnp.zeros((128 - G, H), F32)], 0).astype(BF16)
    ugp = mm_nt(o_hi, w2_hi) + mm_nt(o_lo, w2_hi) + mm_nt(o_hi, w2_lo)
    ugs[...] = ugp.reshape(n, 8, 128)
    rug[me] = ugs[me]
    send(lambda peer: ugs.at[peer], rug.at[me], g_ss, g_rs)

    gt_ref[...] = gt_total
    tg_ref[...] = mm(cgt[...], ubig[...].reshape(R * NU * K, E)) * scale

    for g, (r0, cnt) in enumerate(groups):
        await_all(rz.at[others, pl.ds(r0, cnt)], z_rs.at[g])
        for r in range(r0, r0 + cnt):
            zo_ref[r] = jnp.sum(rz[:, r].astype(F32), 0)
    await_all(rug.at[others], g_rs)
    ugo_ref[...] = jnp.sum(rug[...], 0)
    await_all(ru.at[others], u_ss)
    for g, (r0, cnt) in enumerate(groups):
        await_all(st_in.at[others, pl.ds(r0, cnt)], s_ss.at[g])
        await_all(zs.at[others, pl.ds(r0, cnt)], z_ss.at[g])
    await_all(ugs.at[others], g_ss)


def body(
    n,
    user_emb,
    user_gate,
    item_table,
    item_gate,
    cand_ids,
    positives,
    loss_weight,
    w_in,
    b_in,
    w_out,
    b_out,
):
    R, UL, E = user_emb.shape
    G = user_gate.shape[2]
    NU = positives.shape[1]
    C = cand_ids.shape[1]
    T = item_table.shape[0]
    H, K = w_out.shape
    D = E // K
    assert R * UL == 8 and UL * K == 16 and NU == UL * n
    flat = user_emb.reshape(R * UL, E)
    low = jnp.concatenate([flat[:, : E // 2], jnp.pad(user_gate.reshape(R * UL, G), ((0, 0), (0, 128 - G)))], 1)
    high = jnp.pad(flat[:, E // 2 :], ((0, 0), (0, 128)))
    x = jnp.concatenate([low, high], 0)
    dims = (R, NU, UL, C, T, K, E, G, H)
    vm = pl.BlockSpec(memory_space=pltpu.VMEM)
    dma = pltpu.SemaphoreType.DMA
    z, ug, tg, gt = pl.pallas_call(
        functools.partial(kernel, n, dims),
        out_shape=(
            jax.ShapeDtypeStruct((R, UL * K, D), F32),
            jax.ShapeDtypeStruct((R * UL, 128), F32),
            jax.ShapeDtypeStruct((T, E), F32),
            jax.ShapeDtypeStruct((G, T), F32),
        ),
        in_specs=[vm] * 10,
        out_specs=(vm,) * 4,
        scratch_shapes=[
            pltpu.VMEM((n, 16, E // 2 + 128), BF16),
            pltpu.VMEM((R, NU * K, E), BF16),
            pltpu.VMEM((R, C, E), BF16),
            pltpu.VMEM((R, C, H), F32),
            pltpu.VMEM((R * NU, H), F32),
            pltpu.VMEM((R, NU * K, C), F32),
            pltpu.VMEM((R, NU * K, C), F32),
            pltpu.VMEM((R, NU, C), F32),
            pltpu.VMEM((R, 8, 128), F32),
            pltpu.VMEM((n, R, 8, 128), F32),
            pltpu.VMEM((C, NU * 4 * K), BF16),
            pltpu.VMEM((T, R * NU * K), BF16),
            pltpu.VMEM((C, H), F32),
            pltpu.VMEM((NU, 8, H), F32),
            pltpu.VMEM((R * NU, H), F32),
            pltpu.VMEM((n, R, UL * K, D), BF16),
            pltpu.VMEM((n, R, UL * K, D), BF16),
            pltpu.VMEM((n, 8, 128), F32),
            pltpu.VMEM((n, 8, 128), F32),
            dma,
            dma,
            dma((2,)),
            dma((2,)),
            dma((2,)),
            dma((2,)),
            dma,
            dma,
        ],
        compiler_params=pltpu.CompilerParams(
            collective_id=0, has_side_effects=True, vmem_limit_bytes=60 * 1024 * 1024
        ),
    )(
        x,
        item_table,
        item_gate.T,
        cand_ids,
        positives,
        loss_weight,
        w_in,
        b_in.reshape(1, H),
        w_out.T,
        b_out.reshape(1, K),
    )
    return (
        z.reshape(R, UL, E),
        ug[:, :G].reshape(R, UL, G),
        tg,
        gt.T,
    )


def solution(mesh):
    return jax.shard_map(
        functools.partial(body, mesh.shape["items"]),
        mesh=mesh,
        in_specs=(
            P(None, ("parts", "items"), None),
            P(None, ("parts", "items"), None),
            P(("parts", "items"), None),
            P(("parts", "items"), None),
            P(None, ("parts", "items")),
            P(None, "parts"),
            P(None, "parts"),
            P(),
            P(),
            P(),
            P(),
        ),
        out_specs=(
            P(None, ("parts", "items"), None),
            P(None, ("parts", "items"), None),
            P(("parts", "items"), None),
            P(("parts", "items"), None),
        ),
        check_vma=False,
    )
```
